128 devices in a mesh: section: 8 (over y, core), dp: 16 (over z, x).
Axes of the slice: x: 4, y: 4, z: 4, core: 2. Of those that a mesh axis runs over, the one named last changes fastest.
Arguments:
- layer_input: bfloat16 [8, 6144, 8192], P('section', 'dp'), may hold values from -6 to 6
- value_grad: bfloat16 [8, 6144, 1024], P('section', 'dp'), may hold values from -6 to 6
- frozen_weight: bfloat16 [8, 8192, 1024], P('section', 'dp'), may hold values from -0.0625 to 0.0625
- adapter_down: bfloat16 [8, 32, 8192, 64], P('section', None, 'dp'), may hold values from -0.0625 to 0.0625
- adapter_up: bfloat16 [8, 32, 64, 1024], P('section'), may hold values from -0.75 to 0.75
- group_tenant: int32 [8, 48], P('section'), may hold values from 0 to 31
- slot_tenant: int32 [32], replicated, may hold values from 0 to 31, each once
Outputs:
- upstream: bfloat16 [8, 6144, 8192], P('section', 'dp')
- down_matrix_gradient: float32 [8, 32, 8192, 64], P('section', None, 'dp')
- up_grad: float32 [8, 32, 64, 1024], P('section', 'dp')
The draws below stay inside these ranges and needn't reach their ends.
All inputs are finite; a program needn't handle non-finite values.
Results may differ from the reference program's by a relative error of at most 0.024.
Values may be sent and summed in bfloat16 or wider, within the bound.
No kernel may reach another device: no remote copies, remote signals or barrier semaphores. Data moves between devices by JAX's collectives and lax.ppermute only.
A program may use at most 128 MiB of HBM per device.

```python
import math
import jax
import jax.numpy as jnp
import numpy as np
from jax import lax

MODEL_WIDTH = 8192
KV = 1024
RANK = 64
GROUP_ROWS = 128
GROUPS_DEV = 3
TENANTS = 32
GROUPS = 48
SECTION_ROWS = 6144
SECTIONS = 8
N_DP = 16


def set_ends(array, rng, low, high):
    shape = array.shape
    spot = [jax.random.randint(jax.random.fold_in(rng, axis), (), 0, shape[axis]) for axis in range(len(shape))]
    array = array.at[tuple(spot)].set(low)
    longest = shape.index(max(shape))
    spot[longest] = (spot[longest] + 1) % shape[longest]
    return array.at[tuple(spot)].set(high)


def level_of(rng, extent, cuts, low, largest):
    def one(dim, shards_of):
        heights = jax.random.uniform(jax.random.fold_in(jax.random.fold_in(rng, 6), dim), (shards_of,), jnp.float32, low / len(cuts), largest / len(cuts))
        return jnp.repeat(jnp.exp(heights), extent[dim] // shards_of).reshape((-1,) + (1,) * (len(extent) - dim - 1))

    gain = one(*cuts[0])
    for cut in cuts[1:]:
        gain = gain * one(*cut)
    return gain


def rank_table(amount, lean):
    portions = [(1 << 20) // math.isqrt(standing ** lean) + 1 for standing in range(1, amount + 1)]
    deviation = 1 + sum(portions) // (1 << 30)
    return np.cumsum(np.array([max(1, weight // deviation) for weight in portions]))


def ranked_ids(own_key, shape, number_of, slope):
    table = rank_table(number_of, slope)
    pick = jax.random.randint(jax.random.fold_in(own_key, 1), shape, 0, int(table[number_of - 1]))
    grade = jnp.searchsorted(jnp.asarray(table, jnp.int32), pick, side="right")
    return jax.random.permutation(jax.random.fold_in(own_key, 2), number_of)[grade].astype(jnp.int32)


def normal_values(key, dims, scale, limit, cuts=(), held_as=jnp.bfloat16):
    drawn = scale * jax.random.normal(key, dims, jnp.float32)
    if cuts:
        drawn = drawn * level_of(key, dims, cuts, -0.22, 0.18)
    return jnp.clip(drawn, -limit, limit).astype(held_as)


def setup_inputs(seed: int = 0) -> dict:
    splits = jax.random.split(jax.random.key(seed), 8)
    layer_input = normal_values(splits[0], (SECTIONS, SECTION_ROWS, MODEL_WIDTH), 1.0, 6.0, ((0, 8), (1, 16)))
    value_grad = normal_values(splits[1], (SECTIONS, SECTION_ROWS, KV), 1.0, 6.0, ((0, 8), (1, 16)))
    frozen_weight = normal_values(splits[2], (SECTIONS, MODEL_WIDTH, KV), MODEL_WIDTH ** -0.5, 0.0625, ((0, 8), (1, 16)))
    adapter_down = normal_values(splits[3], (SECTIONS, TENANTS, MODEL_WIDTH, RANK), MODEL_WIDTH ** -0.5, 0.0625, ((0, 8), (2, 16)))
    adapter_up = normal_values(splits[4], (SECTIONS, TENANTS, RANK, KV), RANK ** -0.5, 0.75, ((0, 8),))
    group_tenant = set_ends(ranked_ids(splits[5], (SECTIONS, GROUPS), TENANTS, 2), jax.random.fold_in(splits[5], 3), 0, TENANTS - 1).astype(jnp.int32)
    slot_tenant = jax.random.permutation(splits[6], TENANTS).astype(jnp.int32)
    return {"layer_input": layer_input, "value_grad": value_grad, "frozen_weight": frozen_weight, "adapter_down": adapter_down, "adapter_up": adapter_up, "group_tenant": group_tenant, "slot_tenant": slot_tenant}


adapter_scale = 2.0


def one_section(carry):
    x, dv, w, a, b, tenants = carry
    single_float = jnp.float32
    xg = x.reshape(GROUPS, GROUP_ROWS, MODEL_WIDTH).astype(single_float)
    value_group_gradient = dv.reshape(GROUPS, GROUP_ROWS, KV).astype(single_float)
    adapter_gradient = a[tenants].astype(single_float)
    bg = b[tenants].astype(single_float)
    low_rank_state = jnp.einsum('gnk,grk->gnr', value_group_gradient, bg).astype(jnp.bfloat16)
    frozen_input_gradient = jnp.dot(dv, w.T, preferred_element_type=jnp.float32)
    adapter_input_gradient = jnp.einsum('lfk,lok->lfo', low_rank_state.astype(single_float), adapter_gradient).reshape(SECTION_ROWS, MODEL_WIDTH)
    input_gradient = (frozen_input_gradient + adapter_scale * adapter_input_gradient).astype(jnp.bfloat16)
    tenant_one_hot = (tenants[None, :] == jnp.arange(TENANTS, dtype=jnp.int32)[:, None]).astype(single_float)
    group_wise = jnp.einsum('gnd,gnr->gdr', xg, low_rank_state.astype(single_float))
    down_matrix_gradient = jnp.einsum('pc,cxf->pxf', tenant_one_hot, group_wise, precision=lax.Precision.HIGHEST) * (adapter_scale / GROUP_ROWS)
    low_rank_projection = jnp.einsum('gnd,gdr->gnr', xg, adapter_gradient).astype(jnp.bfloat16)
    group_gradient_part = adapter_scale * jnp.einsum('lma,lmb->lab', low_rank_projection.astype(single_float), value_group_gradient)
    blocks = group_gradient_part.reshape(N_DP, GROUPS_DEV, RANK, KV)
    sel = tenant_one_hot.reshape(TENANTS, N_DP, GROUPS_DEV)
    parts = jnp.einsum('tjc,jcrk->tjrk', sel, blocks, precision=lax.Precision.HIGHEST).astype(jnp.bfloat16)
    parts = lax.optimization_barrier(parts).astype(single_float)
    summed = jnp.sum(parts, axis=1) / GROUP_ROWS
    return input_gradient, down_matrix_gradient, summed


def reference(layer_input, value_grad, frozen_weight, adapter_down, adapter_up, group_tenant, slot_tenant):
    grads, down_matrix_gradient, summed = lax.map(one_section, (layer_input, value_grad, frozen_weight, adapter_down, adapter_up, group_tenant))
    upstream = jnp.concatenate([grads[1:], jnp.zeros_like(grads[:1])], axis=0)
    up_grad = summed[:, slot_tenant]
    return upstream, down_matrix_gradient, up_grad
```

```python
import jax
import jax.numpy as jnp
from jax import lax
from jax.experimental import pallas as pl
from jax.experimental.pallas import tpu as pltpu
from jax.sharding import PartitionSpec as P

GROUP_ROWS = 128
ADAPTER_SCALE = 2.0
RING = 4

F32 = jnp.float32
BF16 = jnp.bfloat16
NT = (((1,), (1,)), ((), ()))
TN = (((0,), (0,)), ((), ()))


def dot(a, b, dims):
    return lax.dot_general(a, b, dims, preferred_element_type=F32)


def cost(flops, nbytes):
    return pl.CostEstimate(flops=int(flops), bytes_accessed=int(nbytes), transcendentals=0)


def to_previous_section(block):
    n = lax.axis_size("section")
    return lax.ppermute(block, "section", [(i, i - 1) for i in range(1, n)])


def along_x(distance):
    return [
        (RING * z + x, RING * z + (x + distance) % RING) for z in range(RING) for x in range(RING)
    ]


def along_z(distance):
    return [
        (RING * z + x, RING * ((z + distance) % RING) + x) for z in range(RING) for x in range(RING)
    ]


def exchange(blocks):
    return lax.all_to_all(blocks, "dp", split_axis=0, concat_axis=0, tiled=True)


def gather_ring(part, first, second):
    n = part.shape[0]
    up = lax.ppermute(part, "dp", first(1))
    down = lax.ppermute(part, "dp", first(-1))
    far_a = lax.ppermute(up[: n // 2], "dp", first(1))
    far_b = lax.ppermute(down[n // 2 :], "dp", first(-1))
    line = jnp.concatenate([part, up, down, far_a, far_b], axis=0)
    m = line.shape[0]
    plane_up = lax.ppermute(line, "dp", second(1))
    plane_down = lax.ppermute(line, "dp", second(-1))
    plane_far_a = lax.ppermute(plane_up[: m // 2], "dp", second(1))
    plane_far_b = lax.ppermute(plane_down[m // 2 :], "dp", second(-1))
    return line, plane_up, plane_down, plane_far_a, plane_far_b


def group_terms(x, low_t):
    rows, width = x.shape
    groups, rank, _ = low_t.shape
    n = lax.axis_size("dp")
    cols = width // n

    def body(x_ref, low_ref, o_ref):
        for g in range(groups):
            o_ref[0, g] = jnp.dot(
                low_ref[g],
                x_ref[g * GROUP_ROWS : (g + 1) * GROUP_ROWS, :],
                preferred_element_type=F32,
            ).astype(BF16)

    return pl.pallas_call(
        body,
        grid=(n,),
        in_specs=[
            pl.BlockSpec((rows, cols), lambda d: (0, d)),
            pl.BlockSpec((groups, rank, GROUP_ROWS), lambda d: (0, 0, 0)),
        ],
        out_specs=pl.BlockSpec((1, groups, rank, cols), lambda d: (d, 0, 0, 0)),
        out_shape=jax.ShapeDtypeStruct((n, groups, rank, cols), BF16),
        cost_estimate=cost(2 * rows * width * rank, 2 * (rows * width + groups * rank * width)),
    )(x, low_t)


def project(x, down):
    rows, width = x.shape
    n, groups, rank, cols = down.shape

    def body(x_ref, a_ref, o_ref, acc):
        d = pl.program_id(0)

        @pl.when(d == 0)
        def _():
            acc[...] = jnp.zeros_like(acc)

        for g in range(groups):
            span = slice(g * GROUP_ROWS, (g + 1) * GROUP_ROWS)
            acc[:, span] += dot(a_ref[0, g], x_ref[span, :], NT)

        @pl.when(d == n - 1)
        def _():
            o_ref[...] = acc[...].astype(BF16)

    return pl.pallas_call(
        body,
        grid=(n,),
        in_specs=[
            pl.BlockSpec((rows, cols), lambda d: (0, d)),
            pl.BlockSpec((1, groups, rank, cols), lambda d: (d, 0, 0, 0)),
        ],
        out_specs=pl.BlockSpec((rank, rows), lambda d: (0, 0)),
        out_shape=jax.ShapeDtypeStruct((rank, rows), BF16),
        scratch_shapes=[pltpu.VMEM((rank, rows), F32)],
        cost_estimate=cost(2 * rows * width * rank, 2 * (rows * width + groups * rank * width)),
    )(x, down)


def sum_by_tenant(parts, tenants, n_tenants):
    n_groups, rank, cols = parts.shape
    steps = 4
    r = rank // steps
    scale = ADAPTER_SCALE / GROUP_ROWS

    def body(t_ref, p_ref, o_ref):
        o_ref[...] = jnp.zeros_like(o_ref)

        @pl.loop(0, n_groups)
        def _(g):
            t = t_ref[g]
            o_ref[t] += p_ref[g].astype(F32) * scale

    return pl.pallas_call(
        body,
        grid_spec=pltpu.PrefetchScalarGridSpec(
            num_scalar_prefetch=1,
            grid=(steps,),
            in_specs=[pl.BlockSpec((n_groups, r, cols), lambda i, t: (0, i, 0))],
            out_specs=pl.BlockSpec((n_tenants, r, cols), lambda i, t: (0, i, 0)),
        ),
        out_shape=jax.ShapeDtypeStruct((n_tenants, rank, cols), F32),
        cost_estimate=cost(
            n_groups * rank * cols, 2 * n_groups * rank * cols + 4 * n_tenants * rank * cols
        ),
    )(tenants, parts)


def up_terms(v_t, proj_t, tenants, slots):
    n, kv, rows = v_t.shape
    rank = proj_t.shape[1]
    groups = rows // GROUP_ROWS
    n_tenants = slots.shape[0]
    per = n_tenants // n

    def body(t_ref, s_ref, v_ref, p_ref, o_ref, acc):
        acc[...] = jnp.zeros_like(acc)

        @pl.loop(0, n)
        def _(d):
            for g in range(groups):
                span = slice(g * GROUP_ROWS, (g + 1) * GROUP_ROWS)
                t = t_ref[d * groups + g]
                acc[t] += dot(v_ref[d, :, span], p_ref[d, :, span], NT)

        for o in range(n):
            for k in range(per):
                o_ref[o, :, k * rank : (k + 1) * rank] = acc[s_ref[o * per + k]].astype(BF16)

    return pl.pallas_call(
        body,
        in_specs=[
            pl.BlockSpec(memory_space=pltpu.SMEM),
            pl.BlockSpec(memory_space=pltpu.SMEM),
            pl.BlockSpec(memory_space=pltpu.VMEM),
            pl.BlockSpec(memory_space=pltpu.VMEM),
        ],
        out_specs=pl.BlockSpec(memory_space=pltpu.VMEM),
        out_shape=jax.ShapeDtypeStruct((n, kv, per * rank), BF16),
        scratch_shapes=[pltpu.VMEM((n_tenants, kv, rank), F32)],
        cost_estimate=cost(2 * n * rows * kv * rank, 4 * n * rows * kv),
    )(tenants, slots, v_t, proj_t)


def gradient_columns(out, blocks, v, weight, low_t, down):
    rows, kv = v.shape
    n, groups, rank, cols = down.shape
    half = cols // 2
    count = weight.shape[0] // half

    def body(b_ref, v_ref, w_ref, low_ref, a_ref, *rest):
        o_ref = rest[-1]
        frozen = dot(v_ref[...], w_ref[...], NT)
        for g in range(groups):
            span = slice(g * GROUP_ROWS, (g + 1) * GROUP_ROWS)
            adapter = dot(low_ref[g], a_ref[0, g], TN)
            o_ref[span, :] = (frozen[span] + ADAPTER_SCALE * adapter).astype(BF16)

    in_specs = [
        pl.BlockSpec((rows, kv), lambda i, b: (0, 0)),
        pl.BlockSpec((half, kv), lambda i, b: (i, 0)),
        pl.BlockSpec((groups, rank, GROUP_ROWS), lambda i, b: (0, 0, 0)),
        pl.BlockSpec((1, groups, rank, half), lambda i, b: (b[i] // 2, 0, 0, b[i] % 2)),
    ]
    args = [blocks, v, weight, low_t, down]
    aliases = {}
    if out is not None:
        in_specs.append(pl.BlockSpec(memory_space=pl.ANY))
        aliases = {len(args): 0}
        args.append(out)
    width = n * cols
    return pl.pallas_call(
        body,
        grid_spec=pltpu.PrefetchScalarGridSpec(
            num_scalar_prefetch=1,
            grid=(count,),
            in_specs=in_specs,
            out_specs=pl.BlockSpec((rows, half), lambda i, b: (0, b[i])),
        ),
        out_shape=jax.ShapeDtypeStruct((rows, width), BF16),
        input_output_aliases=aliases,
        cost_estimate=cost(
            2 * rows * (kv + rank) * half * count, 2 * (rows * kv + count * half * (kv + rows))
        ),
    )(*args)


def local(
    layer_input, value_grad, frozen_weight, adapter_down, adapter_up, group_tenant, slot_tenant
):
    x = layer_input[0]
    v = value_grad[0]
    w = frozen_weight[0]
    down = jnp.swapaxes(adapter_down[0], 1, 2)
    up = adapter_up[0]
    tenants = group_tenant[0]
    n = lax.axis_size("dp")
    me = lax.axis_index("dp")
    rows, kv = v.shape
    n_tenants, rank, cols = down.shape
    groups = rows // GROUP_ROWS
    my_tenants = lax.dynamic_slice_in_dim(tenants, me * groups, groups)

    w_next = to_previous_section(w)
    v_next = to_previous_section(v)

    down_mine = exchange(down[tenants].reshape(n, groups, rank, cols))
    v_t_all = exchange(v.T.reshape(n, kv // n, rows))

    low_t = jnp.einsum(
        "grk,gnk->grn",
        up[my_tenants],
        v.reshape(groups, GROUP_ROWS, kv),
        preferred_element_type=F32,
    ).astype(BF16)
    low_next = to_previous_section(low_t)
    terms = exchange(group_terms(x, low_t))

    half = cols // 2
    ring_a = gather_ring(w_next[:half], along_x, along_z)
    ring_b = gather_ring(w_next[half:], along_z, along_x)

    proj_t = project(x, down_mine)
    down_next = to_previous_section(down_mine)
    proj_all = lax.all_gather(proj_t, "dp", axis=0)
    up_sent = exchange(up_terms(v_t_all, proj_all, tenants, slot_tenant))
    up_grad = (
        up_sent.reshape(kv, -1).T.reshape(-1, rank, kv).astype(F32) * (ADAPTER_SCALE / GROUP_ROWS)
    )

    mz, mx = me // RING, me % RING
    order = (0, -1, 1, 2)

    def ids(first, second, part):
        out = []
        for s in second:
            for f in first:
                dz, dx = (s, f) if part == 0 else (f, s)
                d = RING * ((mz + dz) % RING) + (mx + dx) % RING
                out.append(2 * d + part)
        return jnp.stack(out).astype(jnp.int32)

    out = None
    for piece, (first, second) in enumerate(
        ((order, (0,)), (order, (-1,)), (order, (1,)), (order[:2], (2,)), (order[2:], (2,)))
    ):
        for part, ring in enumerate((ring_a, ring_b)):
            out = gradient_columns(
                out, ids(first, second, part), v_next, ring[piece], low_next, down_next
            )

    down_grad = sum_by_tenant(terms.reshape(n * groups, rank, cols), tenants, n_tenants)
    return (out[None], jnp.swapaxes(down_grad, 1, 2)[None], up_grad[None])


def solution(mesh):
    placed = (
        P("section", "dp", None),
        P("section", "dp", None),
        P("section", "dp", None),
        P("section", None, "dp", None),
        P("section", None, None, None),
        P("section", None),
        P(),
    )
    return jax.shard_map(
        local,
        mesh=mesh,
        in_specs=placed,
        out_specs=(
            P("section", "dp", None),
            P("section", None, "dp", None),
            P("section", "dp", None, None),
        ),
        check_vma=False,
    )
```

```python
import jax
import jax.numpy as jnp
from jax import lax
from jax.experimental import pallas as pl
from jax.experimental.pallas import tpu as pltpu
from jax.sharding import PartitionSpec as P

GROUP_ROWS = 128
ADAPTER_SCALE = 2.0
WIDE = 4
PARAMS = pltpu.CompilerParams(vmem_limit_bytes=48 * 2**20)
RING = 4

F32 = jnp.float32
BF16 = jnp.bfloat16
NT = (((1,), (1,)), ((), ()))


def dot(a, b, dims):
    return lax.dot_general(a, b, dims, preferred_element_type=F32)


def cost(flops, nbytes):
    return pl.CostEstimate(flops=int(flops), bytes_accessed=int(nbytes), transcendentals=0)


def to_previous_section(block):
    n = lax.axis_size("section")
    return lax.ppermute(block, "section", [(i, i - 1) for i in range(1, n)])


def along(axis, distance, down):
    route = []
    for section in range(lax.axis_size("section") - down):
        for z in range(RING):
            for x in range(RING):
                if (axis == "row") == (section % 2 == 0):
                    to = (z, (x + distance) % RING)
                else:
                    to = ((z + distance) % RING, x)
                base = RING * RING * section
                start = base + RING * RING * down + RING * z + x
                route.append((start, base + RING * to[0] + to[1]))
    return route


def move(block, axis, distance, down=0):
    return lax.ppermute(block, ("section", "dp"), along(axis, distance, down))


def exchange(blocks):
    return lax.all_to_all(blocks, "dp", split_axis=0, concat_axis=0, tiled=True)


def together(*values):
    return lax.optimization_barrier(values)


def group_terms(x, low_t):
    rows, width = x.shape
    groups, rank, _ = low_t.shape
    n = lax.axis_size("dp")
    cols = width // n

    def body(x_ref, low_ref, o_ref):
        for q in range(WIDE):
            for g in range(groups):
                o_ref[q, g] = jnp.dot(
                    low_ref[g],
                    x_ref[g * GROUP_ROWS : (g + 1) * GROUP_ROWS, q * cols : (q + 1) * cols],
                    preferred_element_type=F32,
                ).astype(BF16)

    return pl.pallas_call(
        body,
        grid=(n // WIDE,),
        in_specs=[
            pl.BlockSpec((rows, WIDE * cols), lambda d: (0, d)),
            pl.BlockSpec((groups, rank, GROUP_ROWS), lambda d: (0, 0, 0)),
        ],
        out_specs=pl.BlockSpec((WIDE, groups, rank, cols), lambda d: (d, 0, 0, 0)),
        out_shape=jax.ShapeDtypeStruct((n, groups, rank, cols), BF16),
        compiler_params=PARAMS,
        cost_estimate=cost(2 * rows * width * rank, 2 * (rows * width + groups * rank * width)),
    )(x, low_t)


def segments(groups, rank):
    half = groups * rank // 2
    out = []
    for g in range(groups):
        start, stop = g * rank, (g + 1) * rank
        for side in range(2):
            lo, hi = max(start, side * half), min(stop, (side + 1) * half)
            if lo < hi:
                out.append((g, slice(lo - start, hi - start), side, slice(lo - side * half, hi - side * half)))
    return out


def up_parts(x, down, v):
    rows, width = x.shape
    n, groups, rank, cols = down.shape
    kv = v.shape[1]

    def body(x_ref, a_ref, v_ref, o_ref, acc):
        d = pl.program_id(0)

        @pl.when(d == 0)
        def _():
            acc[...] = jnp.zeros_like(acc)

        for g in range(groups):
            span = slice(g * GROUP_ROWS, (g + 1) * GROUP_ROWS)
            for q in range(WIDE):
                acc[:, span] += dot(a_ref[q, g], x_ref[span, q * cols : (q + 1) * cols], NT)

        @pl.when(d == n // WIDE - 1)
        def _():
            for g, term, side, place in segments(groups, rank):
                span = slice(g * GROUP_ROWS, (g + 1) * GROUP_ROWS)
                o_ref[place, side * kv : (side + 1) * kv] = jnp.dot(
                    acc[term, span].astype(BF16), v_ref[span, :], preferred_element_type=F32
                ).astype(BF16)

    return pl.pallas_call(
        body,
        grid=(n // WIDE,),
        in_specs=[
            pl.BlockSpec((rows, WIDE * cols), lambda d: (0, d)),
            pl.BlockSpec((WIDE, groups, rank, cols), lambda d: (d, 0, 0, 0)),
            pl.BlockSpec((rows, kv), lambda d: (0, 0)),
        ],
        out_specs=pl.BlockSpec((groups * rank // 2, 2 * kv), lambda d: (0, 0)),
        out_shape=jax.ShapeDtypeStruct((groups * rank // 2, 2 * kv), BF16),
        scratch_shapes=[pltpu.VMEM((rank, rows), F32)],
        compiler_params=PARAMS,
        cost_estimate=cost(2 * rows * width * rank, 2 * (rows * width + groups * rank * width)),
    )(x, down, v)


def frozen_terms(stacks, weights, tail=None, with_tail=0):
    rows, kv = stacks[0].shape
    width = sum(w.shape[0] for w in weights)
    extra = tail.shape[0] if with_tail else 0
    heights = [rows + (extra if i < with_tail else 0) for i in range(len(stacks))]
    tails = [tail] if with_tail else []

    def body(*refs):
        w_refs, refs = refs[: len(weights)], refs[len(weights) :]
        v_refs, refs = refs[: len(stacks)], refs[len(stacks) :]
        o_refs = refs[len(tails) :]
        for i, (v_ref, o_ref) in enumerate(zip(v_refs, o_refs)):
            left = 0
            for w_ref in w_refs:
                span = slice(left, left + w_ref.shape[0])
                o_ref[:rows, span] = dot(v_ref[...], w_ref[...], NT).astype(BF16)
                left += w_ref.shape[0]
            if i < with_tail:
                o_ref[rows:, :] = refs[0][...]

    def whole(shape):
        return pl.BlockSpec(shape, lambda i: (0, 0))

    return pl.pallas_call(
        body,
        grid=(1,),
        in_specs=[whole(a.shape) for a in (*weights, *stacks, *tails)],
        out_specs=[whole((h, width)) for h in heights],
        out_shape=[jax.ShapeDtypeStruct((h, width), BF16) for h in heights],
        compiler_params=PARAMS,
        cost_estimate=cost(
            2 * sum(heights) * kv * width, 2 * (sum(heights) * (kv + width) + kv * width)
        ),
    )(*weights, *stacks, *tails)


def up_by_slot(pieces, places, slots, rank):
    groups = places.shape[0] // len(pieces)
    height, kv = groups * rank // 2, pieces[0].shape[1] // 2

    def body(place_ref, *refs):
        parts, o_ref, acc = refs[:-2], refs[-2], refs[-1]
        acc[...] = jnp.zeros_like(acc)
        for p, part in enumerate(parts):
            for g, term, side, rows in segments(groups, rank):
                place = place_ref[p * groups + g]

                @pl.when(place < slots)
                def _():
                    acc[place, term] += part[rows, side * kv : (side + 1) * kv].astype(F32)

        o_ref[...] = acc[...].astype(BF16)

    in_specs = [pl.BlockSpec(memory_space=pltpu.SMEM)]
    for piece in pieces:
        last = piece.shape[0] // height - 1
        in_specs.append(pl.BlockSpec((height, 2 * kv), lambda i, last=last: (last, 0)))
    return pl.pallas_call(
        body,
        grid=(1,),
        in_specs=in_specs,
        out_specs=pl.BlockSpec((slots, rank, kv), lambda i: (0, 0, 0)),
        out_shape=jax.ShapeDtypeStruct((slots, rank, kv), BF16),
        scratch_shapes=[pltpu.VMEM((slots, rank, kv), F32)],
        compiler_params=PARAMS,
        cost_estimate=cost(
            len(pieces) * height * kv, 2 * (2 * len(pieces) * height + slots * rank) * kv
        ),
    )(places, *pieces)


def sum_by_tenant(parts, tenants, n_tenants):
    n, groups, rank, cols = parts.shape
    steps = 4
    r = rank // steps
    scale = ADAPTER_SCALE / GROUP_ROWS

    def body(t_ref, p_ref, o_ref):
        o_ref[...] = jnp.zeros_like(o_ref)

        @pl.loop(0, n)
        def _(d):
            for g in range(groups):
                o_ref[t_ref[d * groups + g]] += p_ref[d, g].astype(F32) * scale

    return pl.pallas_call(
        body,
        grid_spec=pltpu.PrefetchScalarGridSpec(
            num_scalar_prefetch=1,
            grid=(steps,),
            in_specs=[pl.BlockSpec((n, groups, r, cols), lambda i, t: (0, 0, i, 0))],
            out_specs=pl.BlockSpec((n_tenants, r, cols), lambda i, t: (0, i, 0)),
        ),
        out_shape=jax.ShapeDtypeStruct((n_tenants, rank, cols), F32),
        cost_estimate=cost(
            n * groups * rank * cols, 2 * n * groups * rank * cols + 4 * n_tenants * rank * cols
        ),
    )(tenants, parts)


def gradient_columns(out, blocks, frozen, low, down):
    n, groups, rank, cols = down.shape
    rows = groups * GROUP_ROWS
    count = frozen.shape[1] // cols

    def body(b_ref, f_ref, low_ref, a_ref, *rest):
        o_ref = rest[-1]
        for g in range(groups):
            span = slice(g * GROUP_ROWS, (g + 1) * GROUP_ROWS)
            adapter = jnp.dot(low_ref[g], a_ref[0, g], preferred_element_type=F32)
            o_ref[span, :] = (f_ref[span, :].astype(F32) + ADAPTER_SCALE * adapter).astype(BF16)

    in_specs = [
        pl.BlockSpec((rows, cols), lambda i, b: (0, i)),
        pl.BlockSpec((groups, GROUP_ROWS, rank), lambda i, b: (0, 0, 0)),
        pl.BlockSpec((1, groups, rank, cols), lambda i, b: (b[i], 0, 0, 0)),
    ]
    args = [blocks, frozen, low, down]
    aliases = {}
    if out is not None:
        in_specs.append(pl.BlockSpec(memory_space=pl.ANY))
        aliases = {len(args): 0}
        args.append(out)
    return pl.pallas_call(
        body,
        grid_spec=pltpu.PrefetchScalarGridSpec(
            num_scalar_prefetch=1,
            grid=(count,),
            in_specs=in_specs,
            out_specs=pl.BlockSpec((rows, cols), lambda i, b: (0, b[i])),
        ),
        out_shape=jax.ShapeDtypeStruct((rows, n * cols), BF16),
        input_output_aliases=aliases,
        cost_estimate=cost(2 * rows * rank * cols * count, 4 * count * rows * cols),
    )(*args)


def local(
    layer_input, value_grad, frozen_weight, adapter_down, adapter_up, group_tenant, slot_tenant
):
    x = layer_input[0]
    v = value_grad[0]
    w = frozen_weight[0]
    down = jnp.swapaxes(adapter_down[0], 1, 2)
    up = adapter_up[0]
    tenants = group_tenant[0]
    n = lax.axis_size("dp")
    me = lax.axis_index("dp")
    rows, kv = v.shape
    n_tenants, rank, cols = down.shape
    groups = rows // GROUP_ROWS
    my_tenants = lax.dynamic_slice_in_dim(tenants, me * groups, groups)

    weights = tuple(move(w, "col", step, 1) for step in (0, 1, -1, 2))
    v_next = to_previous_section(v)

    down_mine = exchange(down[tenants].reshape(n, groups, rank, cols))

    low = jnp.einsum(
        "gnk,grk->gnr",
        v.reshape(groups, GROUP_ROWS, kv),
        up[my_tenants],
        preferred_element_type=F32,
    ).astype(BF16)
    low_next = to_previous_section(low)
    sent = group_terms(x, jnp.swapaxes(low, 1, 2))
    v_below, v_above, v_far = (move(v_next, "row", step) for step in (1, -1, 2))
    x, sent = together(x, sent)

    parts = up_parts(x, down_mine, v)
    parts, low_next = together(parts, low_next)
    down_next = to_previous_section(down_mine)
    for_above, for_below = frozen_terms((v_above, v_below), weights, parts, 2)
    from_below, from_above = move(for_above, "row", 1), move(for_below, "row", -1)
    (for_far,) = frozen_terms((v_far,), weights, parts, 1)
    from_far = move(for_far, "row", 2)
    sent, from_below, from_above, from_far, v_next = together(
        sent, from_below, from_above, from_far, v_next
    )
    terms = exchange(sent)
    (own,) = frozen_terms((v_next,), weights)

    odd = lax.axis_index("section") % 2 == 1
    mz, mx = me // RING, me % RING
    row, col = jnp.where(odd, mz, mx), jnp.where(odd, mx, mz)

    def device_at(r, c):
        return jnp.where(odd, RING * r + c, RING * c + r).astype(jnp.int32)

    steps = jnp.array([0, -1, 1, 2])
    per = n_tenants // n
    holders = device_at((row + steps) % RING, col)
    held = tenants.reshape(n, groups)[holders].reshape(-1)
    owners = device_at(row, (col + steps) % RING)
    wanted = slot_tenant.reshape(n, per)[owners].reshape(-1)
    matches = held[:, None] == wanted[None, :]
    places = jnp.where(jnp.any(matches, 1), jnp.argmax(matches, 1), wanted.shape[0])
    by_slot = up_by_slot(
        (parts, from_below, from_above, from_far),
        places.astype(jnp.int32),
        RING * per,
        rank,
    )
    mine, to_below, to_above, to_far = by_slot.reshape(RING, per, rank, kv)
    from_up = (move(to_below, "col", -1), move(to_above, "col", 1), move(to_far, "col", 2))

    out = None
    for piece, step in ((own, 0), (from_below, -1), (from_above, 1), (from_far, 2)):
        blocks = device_at((row + step) % RING, (col + steps) % RING)
        out = gradient_columns(out, blocks, piece, low_next, down_next)

    out, *from_up = together(out, *from_up)
    up_grad = sum((block.astype(F32) for block in from_up), mine.astype(F32))
    up_grad = up_grad * (ADAPTER_SCALE / GROUP_ROWS)
    out, up_grad, terms = together(out, up_grad, terms)
    down_grad = sum_by_tenant(terms, tenants, n_tenants)
    return (out[None], jnp.swapaxes(down_grad, 1, 2)[None], up_grad[None])


def solution(mesh):
    placed = (
        P("section", "dp", None),
        P("section", "dp", None),
        P("section", "dp", None),
        P("section", None, "dp", None),
        P("section", None, None, None),
        P("section", None),
        P(),
    )
    return jax.shard_map(
        local,
        mesh=mesh,
        in_specs=placed,
        out_specs=(
            P("section", "dp", None),
            P("section", None, "dp", None),
            P("section", "dp", None, None),
        ),
        check_vma=False,
    )
```

```python
import jax
import jax.numpy as jnp
from jax import lax
from jax.experimental import pallas as pl
from jax.experimental.pallas import tpu as pltpu
from jax.sharding import PartitionSpec as P

GROUP_ROWS = 128
ADAPTER_SCALE = 2.0
WIDE = 4
PARAMS = pltpu.CompilerParams(vmem_limit_bytes=58 * 2**20)
RING = 4

F32 = jnp.float32
BF16 = jnp.bfloat16
NT = (((1,), (1,)), ((), ()))


def dot(a, b, dims):
    return lax.dot_general(a, b, dims, preferred_element_type=F32)


def cost(flops, nbytes):
    return pl.CostEstimate(flops=int(flops), bytes_accessed=int(nbytes), transcendentals=0)


def to_previous_section(block):
    n = lax.axis_size("section")
    return lax.ppermute(block, "section", [(i, i - 1) for i in range(1, n)])


def along(axis, distance, down):
    route = []
    for section in range(lax.axis_size("section") - down):
        for z in range(RING):
            for x in range(RING):
                if (axis == "row") == (section % 2 == 0):
                    to = (z, (x + distance) % RING)
                else:
                    to = ((z + distance) % RING, x)
                base = RING * RING * section
                start = base + RING * RING * down + RING * z + x
                route.append((start, base + RING * to[0] + to[1]))
    return route


def move(block, axis, distance, down=0):
    return lax.ppermute(block, ("section", "dp"), along(axis, distance, down))


def exchange(blocks):
    return lax.all_to_all(blocks, "dp", split_axis=0, concat_axis=0, tiled=True)


def together(*values):
    return lax.optimization_barrier(values)


def group_terms(x, low_t):
    rows, width = x.shape
    groups, rank, _ = low_t.shape
    n = lax.axis_size("dp")
    cols = width // n

    def body(x_ref, low_ref, o_ref):
        for q in range(WIDE):
            for g in range(groups):
                o_ref[q, g] = jnp.dot(
                    low_ref[g],
                    x_ref[g * GROUP_ROWS : (g + 1) * GROUP_ROWS, q * cols : (q + 1) * cols],
                    preferred_element_type=F32,
                ).astype(BF16)

    return pl.pallas_call(
        body,
        grid=(n // WIDE,),
        in_specs=[
            pl.BlockSpec((rows, WIDE * cols), lambda d: (0, d)),
            pl.BlockSpec((groups, rank, GROUP_ROWS), lambda d: (0, 0, 0)),
        ],
        out_specs=pl.BlockSpec((WIDE, groups, rank, cols), lambda d: (d, 0, 0, 0)),
        out_shape=jax.ShapeDtypeStruct((n, groups, rank, cols), BF16),
        compiler_params=PARAMS,
        cost_estimate=cost(2 * rows * width * rank, 2 * (rows * width + groups * rank * width)),
    )(x, low_t)


def segments(groups, rank):
    half = groups * rank // 2
    out = []
    for g in range(groups):
        start, stop = g * rank, (g + 1) * rank
        for side in range(2):
            lo, hi = max(start, side * half), min(stop, (side + 1) * half)
            if lo < hi:
                out.append((g, slice(lo - start, hi - start), side, slice(lo - side * half, hi - side * half)))
    return out


def up_parts(x, down, v):
    rows, width = x.shape
    n, groups, rank, cols = down.shape
    kv = v.shape[1]

    def body(x_ref, a_ref, v_ref, o_ref, acc):
        d = pl.program_id(0)

        @pl.when(d == 0)
        def _():
            acc[...] = jnp.zeros_like(acc)

        for g in range(groups):
            span = slice(g * GROUP_ROWS, (g + 1) * GROUP_ROWS)
            for q in range(WIDE):
                acc[:, span] += dot(a_ref[q, g], x_ref[span, q * cols : (q + 1) * cols], NT)

        @pl.when(d == n // WIDE - 1)
        def _():
            for g, term, side, place in segments(groups, rank):
                span = slice(g * GROUP_ROWS, (g + 1) * GROUP_ROWS)
                o_ref[place, side * kv : (side + 1) * kv] = jnp.dot(
                    acc[term, span].astype(BF16), v_ref[span, :], preferred_element_type=F32
                ).astype(BF16)

    return pl.pallas_call(
        body,
        grid=(n // WIDE,),
        in_specs=[
            pl.BlockSpec((rows, WIDE * cols), lambda d: (0, d)),
            pl.BlockSpec((WIDE, groups, rank, cols), lambda d: (d, 0, 0, 0)),
            pl.BlockSpec((rows, kv), lambda d: (0, 0)),
        ],
        out_specs=pl.BlockSpec((groups * rank // 2, 2 * kv), lambda d: (0, 0)),
        out_shape=jax.ShapeDtypeStruct((groups * rank // 2, 2 * kv), BF16),
        scratch_shapes=[pltpu.VMEM((rank, rows), F32)],
        compiler_params=PARAMS,
        cost_estimate=cost(2 * rows * width * rank, 2 * (rows * width + groups * rank * width)),
    )(x, down, v)


def frozen_terms(stacks, weights, tail=None):
    kv = weights[0].shape[1]
    rows = stacks[0].shape[0]
    n_w, n_out = len(weights), len(stacks)
    cols = weights[0].shape[0]
    extra = 0 if tail is None else tail.shape[0]
    height, width = rows + extra, n_w * cols
    tails = [] if tail is None else [tail]

    def body(*refs):
        w_hbm, refs = refs[:n_w], refs[n_w:]
        v_hbm, refs = refs[:n_out], refs[n_out:]
        tail_refs, refs = refs[: len(tails)], refs[len(tails) :]
        out_hbm, refs = refs[:n_out], refs[n_out:]
        w_vmem, v_vmem, out_vmem, w_sem, v_sem, out_sem = refs
        w_loads = [
            pltpu.make_async_copy(w_hbm[q], w_vmem.at[q], w_sem.at[q]) for q in range(n_w)
        ]
        v_loads = [
            pltpu.make_async_copy(v_hbm[i], v_vmem.at[i], v_sem.at[i]) for i in range(n_out)
        ]
        w_loads[0].start()
        for load in v_loads + w_loads[1:2]:
            load.start()
        stores = []
        for q in range(n_w):
            w_loads[q].wait()
            if q + 2 < n_w:
                w_loads[q + 2].start()
            span = slice(q * cols, (q + 1) * cols)
            for i in range(n_out):
                if q == 0:
                    v_loads[i].wait()
                out_vmem[i, q, :rows, :] = dot(v_vmem[i], w_vmem[q], NT).astype(BF16)
                if tail_refs:
                    out_vmem[i, q, rows:, :] = tail_refs[0][:, span]
                store = pltpu.make_async_copy(
                    out_vmem.at[i, q], out_hbm[i].at[:, span], out_sem.at[i, q]
                )
                store.start()
                stores.append(store)
        for store in stores:
            store.wait()

    return pl.pallas_call(
        body,
        in_specs=[pl.BlockSpec(memory_space=pl.ANY)] * (n_w + n_out)
        + [pl.BlockSpec(memory_space=pltpu.VMEM)] * len(tails),
        out_specs=[pl.BlockSpec(memory_space=pl.ANY)] * n_out,
        out_shape=[jax.ShapeDtypeStruct((height, width), BF16)] * n_out,
        scratch_shapes=[
            pltpu.VMEM((n_w, cols, kv), BF16),
            pltpu.VMEM((n_out, rows, kv), BF16),
            pltpu.VMEM((n_out, n_w, height, cols), BF16),
            pltpu.SemaphoreType.DMA((n_w,)),
            pltpu.SemaphoreType.DMA((n_out,)),
            pltpu.SemaphoreType.DMA((n_out, n_w)),
        ],
        compiler_params=PARAMS,
        cost_estimate=cost(
            2 * n_out * height * kv * width, 2 * (n_out * height * (kv + width) + kv * width)
        ),
    )(*weights, *stacks, *tails)


def up_by_slot(pieces, places, slots, rank):
    groups = places.shape[0] // len(pieces)
    height, kv = groups * rank // 2, pieces[0].shape[1] // 2

    def body(place_ref, *refs):
        parts, o_ref, acc = refs[:-2], refs[-2], refs[-1]
        acc[...] = jnp.zeros_like(acc)
        for p, part in enumerate(parts):
            for g, term, side, rows in segments(groups, rank):
                place = place_ref[p * groups + g]

                @pl.when(place < slots)
                def _():
                    acc[place, term] += part[rows, side * kv : (side + 1) * kv].astype(F32)

        o_ref[...] = acc[...].astype(BF16)

    in_specs = [pl.BlockSpec(memory_space=pltpu.SMEM)]
    for piece in pieces:
        last = piece.shape[0] // height - 1
        in_specs.append(pl.BlockSpec((height, 2 * kv), lambda i, last=last: (last, 0)))
    return pl.pallas_call(
        body,
        grid=(1,),
        in_specs=in_specs,
        out_specs=pl.BlockSpec((slots, rank, kv), lambda i: (0, 0, 0)),
        out_shape=jax.ShapeDtypeStruct((slots, rank, kv), BF16),
        scratch_shapes=[pltpu.VMEM((slots, rank, kv), F32)],
        compiler_params=PARAMS,
        cost_estimate=cost(
            len(pieces) * height * kv, 2 * (2 * len(pieces) * height + slots * rank) * kv
        ),
    )(places, *pieces)


def sum_by_tenant(parts, tenants, n_tenants):
    n, groups, rank, cols = parts.shape
    steps = 2
    r = rank // steps
    scale = ADAPTER_SCALE / GROUP_ROWS

    def body(t_ref, p_ref, o_ref):
        o_ref[...] = jnp.zeros_like(o_ref)

        @pl.loop(0, n)
        def _(d):
            for g in range(groups):
                o_ref[t_ref[d * groups + g]] += p_ref[d, g].astype(F32) * scale

    return pl.pallas_call(
        body,
        grid_spec=pltpu.PrefetchScalarGridSpec(
            num_scalar_prefetch=1,
            grid=(steps,),
            in_specs=[pl.BlockSpec((n, groups, r, cols), lambda i, t: (0, 0, i, 0))],
            out_specs=pl.BlockSpec((n_tenants, r, cols), lambda i, t: (0, i, 0)),
        ),
        out_shape=jax.ShapeDtypeStruct((n_tenants, rank, cols), F32),
        compiler_params=PARAMS,
        cost_estimate=cost(
            n * groups * rank * cols, 2 * n * groups * rank * cols + 4 * n_tenants * rank * cols
        ),
    )(tenants, parts)


def input_gradient(pieces, blocks, low, down):
    n, groups, rank, cols = down.shape
    per = n // len(pieces)
    width = n * cols

    def body(b_ref, low_ref, a_ref, *refs):
        o_ref = refs[-1]
        for p, f_ref in enumerate(refs[:-1]):
            for i in range(per):
                block = b_ref[p * per + i]
                adapter = jnp.dot(low_ref[0], a_ref[block, 0], preferred_element_type=F32)
                place = pl.ds(pl.multiple_of(block * cols, cols), cols)
                frozen = f_ref[:, i * cols : (i + 1) * cols].astype(F32)
                o_ref[:, place] = (frozen + ADAPTER_SCALE * adapter).astype(BF16)

    return pl.pallas_call(
        body,
        grid_spec=pltpu.PrefetchScalarGridSpec(
            num_scalar_prefetch=1,
            grid=(groups,),
            in_specs=[
                pl.BlockSpec((1, GROUP_ROWS, rank), lambda g, b: (g, 0, 0)),
                pl.BlockSpec((n, 1, rank, cols), lambda g, b: (0, g, 0, 0)),
            ]
            + [pl.BlockSpec((GROUP_ROWS, per * cols), lambda g, b: (g, 0)) for _ in pieces],
            out_specs=pl.BlockSpec((GROUP_ROWS, width), lambda g, b: (g, 0)),
        ),
        out_shape=jax.ShapeDtypeStruct((groups * GROUP_ROWS, width), BF16),
        compiler_params=PARAMS,
        cost_estimate=cost(
            2 * groups * GROUP_ROWS * rank * width,
            2 * groups * (2 * GROUP_ROWS + rank) * width,
        ),
    )(blocks, low, down, *pieces)


def local(
    layer_input, value_grad, frozen_weight, adapter_down, adapter_up, group_tenant, slot_tenant
):
    x = layer_input[0]
    v = value_grad[0]
    w = frozen_weight[0]
    down = jnp.swapaxes(adapter_down[0], 1, 2)
    up = adapter_up[0]
    tenants = group_tenant[0]
    n = lax.axis_size("dp")
    me = lax.axis_index("dp")
    rows, kv = v.shape
    n_tenants, rank, cols = down.shape
    groups = rows // GROUP_ROWS
    my_tenants = lax.dynamic_slice_in_dim(tenants, me * groups, groups)

    weights = tuple(move(w, "col", step, 1) for step in (0, 1, -1, 2))
    v_next = to_previous_section(v)

    down_mine = exchange(down[tenants].reshape(n, groups, rank, cols))

    low = jnp.einsum(
        "gnk,grk->gnr",
        v.reshape(groups, GROUP_ROWS, kv),
        up[my_tenants],
        preferred_element_type=F32,
    ).astype(BF16)
    v_below, v_above, v_far = (move(v_next, "row", step) for step in (1, -1, 2))
    parts = up_parts(x, down_mine, v)
    for_above, for_below = frozen_terms((v_above, v_below), weights, parts)
    from_below, from_above = move(for_above, "row", 1), move(for_below, "row", -1)
    (for_far,) = frozen_terms((v_far,), weights, parts)
    down_mine, low, for_above = together(down_mine, low, for_above)
    down_next = to_previous_section(down_mine)
    low_next = to_previous_section(low)
    from_far = move(for_far, "row", 2)
    low, for_far = together(low, for_far)
    sent = group_terms(x, jnp.swapaxes(low, 1, 2))
    (own,) = frozen_terms((v_next,), weights)
    sent, from_below, from_above, from_far, own = together(
        sent, from_below, from_above, from_far, own
    )
    terms = exchange(sent)

    odd = lax.axis_index("section") % 2 == 1
    mz, mx = me // RING, me % RING
    row, col = jnp.where(odd, mz, mx), jnp.where(odd, mx, mz)

    def device_at(r, c):
        return jnp.where(odd, RING * r + c, RING * c + r).astype(jnp.int32)

    steps = jnp.array([0, -1, 1, 2])
    per = n_tenants // n
    holders = device_at((row + steps) % RING, col)
    held = tenants.reshape(n, groups)[holders].reshape(-1)
    owners = device_at(row, (col + steps) % RING)
    wanted = slot_tenant.reshape(n, per)[owners].reshape(-1)
    matches = held[:, None] == wanted[None, :]
    places = jnp.where(jnp.any(matches, 1), jnp.argmax(matches, 1), wanted.shape[0])
    by_slot = up_by_slot(
        (parts, from_below, from_above, from_far),
        places.astype(jnp.int32),
        RING * per,
        rank,
    )
    mine, to_below, to_above, to_far = by_slot.reshape(RING, per, rank, kv)
    from_up = (move(to_below, "col", -1), move(to_above, "col", 1), move(to_far, "col", 2))

    blocks = jnp.concatenate(
        [device_at((row + step) % RING, (col + steps) % RING) for step in (0, -1, 1, 2)]
    )
    out = input_gradient((own, from_below, from_above, from_far), blocks, low_next, down_next)
    out, *from_up = together(out, *from_up)
    up_grad = sum((block.astype(F32) for block in from_up), mine.astype(F32))
    up_grad = up_grad * (ADAPTER_SCALE / GROUP_ROWS)
    out, up_grad, terms = together(out, up_grad, terms)
    down_grad = sum_by_tenant(terms, tenants, n_tenants)
    return (out[None], jnp.swapaxes(down_grad, 1, 2)[None], up_grad[None])


def solution(mesh):
    placed = (
        P("section", "dp", None),
        P("section", "dp", None),
        P("section", "dp", None),
        P("section", None, "dp", None),
        P("section", None, None, None),
        P("section", None),
        P(),
    )
    return jax.shard_map(
        local,
        mesh=mesh,
        in_specs=placed,
        out_specs=(
            P("section", "dp", None),
            P("section", None, "dp", None),
            P("section", "dp", None, None),
        ),
        check_vma=False,
    )
```

```python
import jax
import jax.numpy as jnp
from jax import lax
from jax.experimental import pallas as pl
from jax.experimental.pallas import tpu as pltpu
from jax.sharding import PartitionSpec as P

GROUP_ROWS = 128
ADAPTER_SCALE = 2.0
WIDE = 4
PARAMS = pltpu.CompilerParams(vmem_limit_bytes=58 * 2**20)
RING = 4

F32 = jnp.float32
BF16 = jnp.bfloat16
NT = (((1,), (1,)), ((), ()))


def dot(a, b, dims):
    return lax.dot_general(a, b, dims, preferred_element_type=F32)


def cost(flops, nbytes):
    return pl.CostEstimate(flops=int(flops), bytes_accessed=int(nbytes), transcendentals=0)


def to_previous_section(block):
    n = lax.axis_size("section")
    return lax.ppermute(block, "section", [(i, i - 1) for i in range(1, n)])


def along(axis, distance, down):
    route = []
    for section in range(lax.axis_size("section") - down):
        for z in range(RING):
            for x in range(RING):
                if (axis == "row") == (section % 2 == 0):
                    to = (z, (x + distance) % RING)
                else:
                    to = ((z + distance) % RING, x)
                base = RING * RING * section
                start = base + RING * RING * down + RING * z + x
                route.append((start, base + RING * to[0] + to[1]))
    return route


def move(block, axis, distance, down=0):
    return lax.ppermute(block, ("section", "dp"), along(axis, distance, down))


def exchange(blocks):
    return lax.all_to_all(blocks, "dp", split_axis=0, concat_axis=0, tiled=True)


def together(*values):
    return lax.optimization_barrier(values)


def group_terms(x, low_t):
    rows, width = x.shape
    groups, rank, _ = low_t.shape
    n = lax.axis_size("dp")
    cols = width // n

    def body(x_ref, low_ref, o_ref):
        for q in range(WIDE):
            for g in range(groups):
                o_ref[q, g] = jnp.dot(
                    low_ref[g],
                    x_ref[g * GROUP_ROWS : (g + 1) * GROUP_ROWS, q * cols : (q + 1) * cols],
                    preferred_element_type=F32,
                ).astype(BF16)

    return pl.pallas_call(
        body,
        grid=(n // WIDE,),
        in_specs=[
            pl.BlockSpec((rows, WIDE * cols), lambda d: (0, d)),
            pl.BlockSpec((groups, rank, GROUP_ROWS), lambda d: (0, 0, 0)),
        ],
        out_specs=pl.BlockSpec((WIDE, groups, rank, cols), lambda d: (d, 0, 0, 0)),
        out_shape=jax.ShapeDtypeStruct((n, groups, rank, cols), BF16),
        compiler_params=PARAMS,
        cost_estimate=cost(2 * rows * width * rank, 2 * (rows * width + groups * rank * width)),
    )(x, low_t)


def segments(groups, rank):
    half = groups * rank // 2
    out = []
    for g in range(groups):
        start, stop = g * rank, (g + 1) * rank
        for side in range(2):
            lo, hi = max(start, side * half), min(stop, (side + 1) * half)
            if lo < hi:
                out.append((g, slice(lo - start, hi - start), side, slice(lo - side * half, hi - side * half)))
    return out


def up_parts(x, down, v):
    rows, width = x.shape
    n, groups, rank, cols = down.shape
    kv = v.shape[1]

    def body(x_ref, a_ref, v_ref, o_ref, acc):
        d = pl.program_id(0)

        @pl.when(d == 0)
        def _():
            acc[...] = jnp.zeros_like(acc)

        for g in range(groups):
            span = slice(g * GROUP_ROWS, (g + 1) * GROUP_ROWS)
            for q in range(WIDE):
                acc[:, span] += dot(a_ref[q, g], x_ref[span, q * cols : (q + 1) * cols], NT)

        @pl.when(d == n // WIDE - 1)
        def _():
            for g, term, side, place in segments(groups, rank):
                span = slice(g * GROUP_ROWS, (g + 1) * GROUP_ROWS)
                o_ref[place, side * kv : (side + 1) * kv] = jnp.dot(
                    acc[term, span].astype(BF16), v_ref[span, :], preferred_element_type=F32
                ).astype(BF16)

    return pl.pallas_call(
        body,
        grid=(n // WIDE,),
        in_specs=[
            pl.BlockSpec((rows, WIDE * cols), lambda d: (0, d)),
            pl.BlockSpec((WIDE, groups, rank, cols), lambda d: (d, 0, 0, 0)),
            pl.BlockSpec((rows, kv), lambda d: (0, 0)),
        ],
        out_specs=pl.BlockSpec((groups * rank // 2, 2 * kv), lambda d: (0, 0)),
        out_shape=jax.ShapeDtypeStruct((groups * rank // 2, 2 * kv), BF16),
        scratch_shapes=[pltpu.VMEM((rank, rows), F32)],
        compiler_params=PARAMS,
        cost_estimate=cost(2 * rows * width * rank, 2 * (rows * width + groups * rank * width)),
    )(x, down, v)


def frozen_terms(stacks, weights, tail=None):
    kv = weights[0].shape[1]
    rows = stacks[0].shape[0]
    n_w, n_out = len(weights), len(stacks)
    cols = weights[0].shape[0]
    extra = 0 if tail is None else tail.shape[0]
    height, width = rows + extra, n_w * cols
    tails = [] if tail is None else [tail]

    def body(*refs):
        w_hbm, refs = refs[:n_w], refs[n_w:]
        v_hbm, refs = refs[:n_out], refs[n_out:]
        tail_refs, refs = refs[: len(tails)], refs[len(tails) :]
        out_hbm, refs = refs[:n_out], refs[n_out:]
        w_vmem, v_vmem, out_vmem, w_sem, v_sem, out_sem = refs
        w_loads = [
            pltpu.make_async_copy(w_hbm[q], w_vmem.at[q], w_sem.at[q]) for q in range(n_w)
        ]
        v_loads = [
            pltpu.make_async_copy(v_hbm[i], v_vmem.at[i], v_sem.at[i]) for i in range(n_out)
        ]
        w_loads[0].start()
        for load in v_loads + w_loads[1:2]:
            load.start()
        stores = []
        for q in range(n_w):
            w_loads[q].wait()
            if q + 2 < n_w:
                w_loads[q + 2].start()
            span = slice(q * cols, (q + 1) * cols)
            for i in range(n_out):
                if q == 0:
                    v_loads[i].wait()
                out_vmem[i, q, :rows, :] = dot(v_vmem[i], w_vmem[q], NT).astype(BF16)
                if tail_refs:
                    out_vmem[i, q, rows:, :] = tail_refs[0][:, span]
                store = pltpu.make_async_copy(
                    out_vmem.at[i, q], out_hbm[i].at[:, span], out_sem.at[i, q]
                )
                store.start()
                stores.append(store)
        for store in stores:
            store.wait()

    return pl.pallas_call(
        body,
        in_specs=[pl.BlockSpec(memory_space=pl.ANY)] * (n_w + n_out)
        + [pl.BlockSpec(memory_space=pltpu.VMEM)] * len(tails),
        out_specs=[pl.BlockSpec(memory_space=pl.ANY)] * n_out,
        out_shape=[jax.ShapeDtypeStruct((height, width), BF16)] * n_out,
        scratch_shapes=[
            pltpu.VMEM((n_w, cols, kv), BF16),
            pltpu.VMEM((n_out, rows, kv), BF16),
            pltpu.VMEM((n_out, n_w, height, cols), BF16),
            pltpu.SemaphoreType.DMA((n_w,)),
            pltpu.SemaphoreType.DMA((n_out,)),
            pltpu.SemaphoreType.DMA((n_out, n_w)),
        ],
        compiler_params=PARAMS,
        cost_estimate=cost(
            2 * n_out * height * kv * width, 2 * (n_out * height * (kv + width) + kv * width)
        ),
    )(*weights, *stacks, *tails)


def up_by_slot(pieces, places, slots, rank):
    groups = places.shape[0] // len(pieces)
    height, kv = groups * rank // 2, pieces[0].shape[1] // 2

    def body(place_ref, *refs):
        parts, o_ref, acc = refs[:-2], refs[-2], refs[-1]
        acc[...] = jnp.zeros_like(acc)
        for p, part in enumerate(parts):
            for g, term, side, rows in segments(groups, rank):
                place = place_ref[p * groups + g]

                @pl.when(place < slots)
                def _():
                    acc[place, term] += part[rows, side * kv : (side + 1) * kv].astype(F32)

        o_ref[...] = acc[...].astype(BF16)

    in_specs = [pl.BlockSpec(memory_space=pltpu.SMEM)]
    for piece in pieces:
        last = piece.shape[0] // height - 1
        in_specs.append(pl.BlockSpec((height, 2 * kv), lambda i, last=last: (last, 0)))
    return pl.pallas_call(
        body,
        grid=(1,),
        in_specs=in_specs,
        out_specs=pl.BlockSpec((slots, rank, kv), lambda i: (0, 0, 0)),
        out_shape=jax.ShapeDtypeStruct((slots, rank, kv), BF16),
        scratch_shapes=[pltpu.VMEM((slots, rank, kv), F32)],
        compiler_params=PARAMS,
        cost_estimate=cost(
            len(pieces) * height * kv, 2 * (2 * len(pieces) * height + slots * rank) * kv
        ),
    )(places, *pieces)


def sum_by_tenant(parts, tenants, n_tenants):
    n, groups, rank, cols = parts.shape
    steps = 2
    r = rank // steps
    scale = ADAPTER_SCALE / GROUP_ROWS

    def body(t_ref, p_ref, o_ref):
        o_ref[...] = jnp.zeros_like(o_ref)

        @pl.loop(0, n)
        def _(d):
            for g in range(groups):
                o_ref[t_ref[d * groups + g]] += p_ref[d, g].astype(F32) * scale

    return pl.pallas_call(
        body,
        grid_spec=pltpu.PrefetchScalarGridSpec(
            num_scalar_prefetch=1,
            grid=(steps,),
            in_specs=[pl.BlockSpec((n, groups, r, cols), lambda i, t: (0, 0, i, 0))],
            out_specs=pl.BlockSpec((n_tenants, r, cols), lambda i, t: (0, i, 0)),
        ),
        out_shape=jax.ShapeDtypeStruct((n_tenants, rank, cols), F32),
        compiler_params=PARAMS,
        cost_estimate=cost(
            n * groups * rank * cols, 2 * n * groups * rank * cols + 4 * n_tenants * rank * cols
        ),
    )(tenants, parts)


def input_gradient(pieces, blocks, low, down):
    n, groups, rank, cols = down.shape
    per = n // len(pieces)
    width = n * cols

    def body(b_ref, low_ref, a_ref, *refs):
        o_ref = refs[-1]
        for p, f_ref in enumerate(refs[:-1]):
            for i in range(per):
                block = b_ref[p * per + i]
                adapter = jnp.dot(low_ref[0], a_ref[block, 0], preferred_element_type=F32)
                place = pl.ds(pl.multiple_of(block * cols, cols), cols)
                frozen = f_ref[:, i * cols : (i + 1) * cols].astype(F32)
                o_ref[:, place] = (frozen + ADAPTER_SCALE * adapter).astype(BF16)

    return pl.pallas_call(
        body,
        grid_spec=pltpu.PrefetchScalarGridSpec(
            num_scalar_prefetch=1,
            grid=(groups,),
            in_specs=[
                pl.BlockSpec((1, GROUP_ROWS, rank), lambda g, b: (g, 0, 0)),
                pl.BlockSpec((n, 1, rank, cols), lambda g, b: (0, g, 0, 0)),
            ]
            + [pl.BlockSpec((GROUP_ROWS, per * cols), lambda g, b: (g, 0)) for _ in pieces],
            out_specs=pl.BlockSpec((GROUP_ROWS, width), lambda g, b: (g, 0)),
        ),
        out_shape=jax.ShapeDtypeStruct((groups * GROUP_ROWS, width), BF16),
        compiler_params=PARAMS,
        cost_estimate=cost(
            2 * groups * GROUP_ROWS * rank * width,
            2 * groups * (2 * GROUP_ROWS + rank) * width,
        ),
    )(blocks, low, down, *pieces)


def local(
    layer_input, value_grad, frozen_weight, adapter_down, adapter_up, group_tenant, slot_tenant
):
    x = layer_input[0]
    v = value_grad[0]
    w = frozen_weight[0]
    down = jnp.swapaxes(adapter_down[0], 1, 2)
    up = adapter_up[0]
    tenants = group_tenant[0]
    n = lax.axis_size("dp")
    me = lax.axis_index("dp")
    rows, kv = v.shape
    n_tenants, rank, cols = down.shape
    groups = rows // GROUP_ROWS
    my_tenants = lax.dynamic_slice_in_dim(tenants, me * groups, groups)

    w_own, w_below, w_above = (move(w, "col", step, 1) for step in (0, 1, -1))
    weights = (w_own, w_below, w_above, move(w_own, "col", 2))
    v_next = to_previous_section(v)

    down_mine = exchange(down[tenants].reshape(n, groups, rank, cols))

    low = jnp.einsum(
        "gnk,grk->gnr",
        v.reshape(groups, GROUP_ROWS, kv),
        up[my_tenants],
        preferred_element_type=F32,
    ).astype(BF16)
    v_below, v_above, v_far = (move(v_next, "row", step) for step in (1, -1, 2))
    parts = up_parts(x, down_mine, v)
    for_above, for_below = frozen_terms((v_above, v_below), weights, parts)
    from_below, from_above = move(for_above, "row", 1), move(for_below, "row", -1)
    (for_far,) = frozen_terms((v_far,), weights, parts)
    low, for_above = together(low, for_above)
    low_next = to_previous_section(low)
    down_mine, low_next = together(down_mine, low_next)
    down_next = to_previous_section(down_mine)
    from_far = move(for_far, "row", 2)
    low, for_far = together(low, for_far)
    sent = group_terms(x, jnp.swapaxes(low, 1, 2))
    (own,) = frozen_terms((v_next,), weights)
    sent, from_below, from_above, from_far, own = together(
        sent, from_below, from_above, from_far, own
    )
    terms = exchange(sent)

    odd = lax.axis_index("section") % 2 == 1
    mz, mx = me // RING, me % RING
    row, col = jnp.where(odd, mz, mx), jnp.where(odd, mx, mz)

    def device_at(r, c):
        return jnp.where(odd, RING * r + c, RING * c + r).astype(jnp.int32)

    steps = jnp.array([0, -1, 1, 2])
    per = n_tenants // n
    holders = device_at((row + steps) % RING, col)
    held = tenants.reshape(n, groups)[holders].reshape(-1)
    owners = device_at(row, (col + steps) % RING)
    wanted = slot_tenant.reshape(n, per)[owners].reshape(-1)
    matches = held[:, None] == wanted[None, :]
    places = jnp.where(jnp.any(matches, 1), jnp.argmax(matches, 1), wanted.shape[0])
    by_slot = up_by_slot(
        (parts, from_below, from_above, from_far),
        places.astype(jnp.int32),
        RING * per,
        rank,
    )
    mine, to_below, to_above, to_far = by_slot.reshape(RING, per, rank, kv)
    from_up = (move(to_below, "col", -1), move(to_above, "col", 1), move(to_far, "col", 2))

    blocks = jnp.concatenate(
        [device_at((row + step) % RING, (col + steps) % RING) for step in (0, -1, 1, 2)]
    )
    out = input_gradient((own, from_below, from_above, from_far), blocks, low_next, down_next)
    out, *from_up = together(out, *from_up)
    up_grad = sum((block.astype(F32) for block in from_up), mine.astype(F32))
    up_grad = up_grad * (ADAPTER_SCALE / GROUP_ROWS)
    out, up_grad, terms = together(out, up_grad, terms)
    down_grad = sum_by_tenant(terms, tenants, n_tenants)
    return (out[None], jnp.swapaxes(down_grad, 1, 2)[None], up_grad[None])


def solution(mesh):
    placed = (
        P("section", "dp", None),
        P("section", "dp", None),
        P("section", "dp", None),
        P("section", None, "dp", None),
        P("section", None, None, None),
        P("section", None),
        P(),
    )
    return jax.shard_map(
        local,
        mesh=mesh,
        in_specs=placed,
        out_specs=(
            P("section", "dp", None),
            P("section", None, "dp", None),
            P("section", "dp", None, None),
        ),
        check_vma=False,
    )
```

```python
import jax
import jax.numpy as jnp
from jax import lax
from jax.experimental import pallas as pl
from jax.experimental.pallas import tpu as pltpu
from jax.sharding import PartitionSpec as P

GROUP_ROWS = 128
ADAPTER_SCALE = 2.0
WIDE = 4
PARAMS = pltpu.CompilerParams(vmem_limit_bytes=58 * 2**20)
RING = 4

F32 = jnp.float32
BF16 = jnp.bfloat16
NT = (((1,), (1,)), ((), ()))


def dot(a, b, dims):
    return lax.dot_general(a, b, dims, preferred_element_type=F32)


def cost(flops, nbytes):
    return pl.CostEstimate(flops=int(flops), bytes_accessed=int(nbytes), transcendentals=0)


def to_previous_section(block):
    n = lax.axis_size("section")
    return lax.ppermute(block, "section", [(i, i - 1) for i in range(1, n)])


def along(axis, distance, down):
    route = []
    for section in range(lax.axis_size("section") - down):
        for z in range(RING):
            for x in range(RING):
                if (axis == "row") == (section % 2 == 0):
                    to = (z, (x + distance) % RING)
                else:
                    to = ((z + distance) % RING, x)
                base = RING * RING * section
                start = base + RING * RING * down + RING * z + x
                route.append((start, base + RING * to[0] + to[1]))
    return route


def move(block, axis, distance, down=0):
    return lax.ppermute(block, ("section", "dp"), along(axis, distance, down))


def exchange(blocks):
    return lax.all_to_all(blocks, "dp", split_axis=0, concat_axis=0, tiled=True)


def together(*values):
    return lax.optimization_barrier(values)


def group_terms(x, low_t):
    rows, width = x.shape
    groups, rank, _ = low_t.shape
    n = lax.axis_size("dp")
    cols = width // n

    def body(x_ref, low_ref, o_ref):
        for q in range(WIDE):
            for g in range(groups):
                o_ref[q, g] = jnp.dot(
                    low_ref[g],
                    x_ref[g * GROUP_ROWS : (g + 1) * GROUP_ROWS, q * cols : (q + 1) * cols],
                    preferred_element_type=F32,
                ).astype(BF16)

    return pl.pallas_call(
        body,
        grid=(n // WIDE,),
        in_specs=[
            pl.BlockSpec((rows, WIDE * cols), lambda d: (0, d)),
            pl.BlockSpec((groups, rank, GROUP_ROWS), lambda d: (0, 0, 0)),
        ],
        out_specs=pl.BlockSpec((WIDE, groups, rank, cols), lambda d: (d, 0, 0, 0)),
        out_shape=jax.ShapeDtypeStruct((n, groups, rank, cols), BF16),
        compiler_params=PARAMS,
        cost_estimate=cost(2 * rows * width * rank, 2 * (rows * width + groups * rank * width)),
    )(x, low_t)


def segments(groups, rank):
    half = groups * rank // 2
    out = []
    for g in range(groups):
        start, stop = g * rank, (g + 1) * rank
        for side in range(2):
            lo, hi = max(start, side * half), min(stop, (side + 1) * half)
            if lo < hi:
                out.append((g, slice(lo - start, hi - start), side, slice(lo - side * half, hi - side * half)))
    return out


def up_parts(x, down, v):
    rows, width = x.shape
    n, groups, rank, cols = down.shape
    kv = v.shape[1]

    def body(x_ref, a_ref, v_ref, o_ref, acc):
        d = pl.program_id(0)

        @pl.when(d == 0)
        def _():
            acc[...] = jnp.zeros_like(acc)

        for g in range(groups):
            span = slice(g * GROUP_ROWS, (g + 1) * GROUP_ROWS)
            for q in range(WIDE):
                acc[:, span] += dot(a_ref[q, g], x_ref[span, q * cols : (q + 1) * cols], NT)

        @pl.when(d == n // WIDE - 1)
        def _():
            for g, term, side, place in segments(groups, rank):
                span = slice(g * GROUP_ROWS, (g + 1) * GROUP_ROWS)
                o_ref[place, side * kv : (side + 1) * kv] = jnp.dot(
                    acc[term, span].astype(BF16), v_ref[span, :], preferred_element_type=F32
                ).astype(BF16)

    return pl.pallas_call(
        body,
        grid=(n // WIDE,),
        in_specs=[
            pl.BlockSpec((rows, WIDE * cols), lambda d: (0, d)),
            pl.BlockSpec((WIDE, groups, rank, cols), lambda d: (d, 0, 0, 0)),
            pl.BlockSpec((rows, kv), lambda d: (0, 0)),
        ],
        out_specs=pl.BlockSpec((groups * rank // 2, 2 * kv), lambda d: (0, 0)),
        out_shape=jax.ShapeDtypeStruct((groups * rank // 2, 2 * kv), BF16),
        scratch_shapes=[pltpu.VMEM((rank, rows), F32)],
        compiler_params=PARAMS,
        cost_estimate=cost(2 * rows * width * rank, 2 * (rows * width + groups * rank * width)),
    )(x, down, v)


def frozen_terms(stacks, weights, tail=None):
    kv = weights[0].shape[1]
    rows = stacks[0].shape[0]
    n_w, n_out = len(weights), len(stacks)
    cols = weights[0].shape[0]
    extra = 0 if tail is None else tail.shape[0]
    height, width = rows + extra, n_w * cols
    tails = [] if tail is None else [tail]

    def body(*refs):
        w_hbm, refs = refs[:n_w], refs[n_w:]
        v_hbm, refs = refs[:n_out], refs[n_out:]
        tail_refs, refs = refs[: len(tails)], refs[len(tails) :]
        out_hbm, refs = refs[:n_out], refs[n_out:]
        w_vmem, v_vmem, out_vmem, w_sem, v_sem, out_sem = refs
        w_loads = [
            pltpu.make_async_copy(w_hbm[q], w_vmem.at[q], w_sem.at[q]) for q in range(n_w)
        ]
        v_loads = [
            pltpu.make_async_copy(v_hbm[i], v_vmem.at[i], v_sem.at[i]) for i in range(n_out)
        ]
        w_loads[0].start()
        for load in v_loads + w_loads[1:2]:
            load.start()
        stores = []
        for q in range(n_w):
            w_loads[q].wait()
            if q + 2 < n_w:
                w_loads[q + 2].start()
            span = slice(q * cols, (q + 1) * cols)
            for i in range(n_out):
                if q == 0:
                    v_loads[i].wait()
                out_vmem[i, q, :rows, :] = dot(v_vmem[i], w_vmem[q], NT).astype(BF16)
                if tail_refs:
                    out_vmem[i, q, rows:, :] = tail_refs[0][:, span]
                store = pltpu.make_async_copy(
                    out_vmem.at[i, q], out_hbm[i].at[:, span], out_sem.at[i, q]
                )
                store.start()
                stores.append(store)
        for store in stores:
            store.wait()

    return pl.pallas_call(
        body,
        in_specs=[pl.BlockSpec(memory_space=pl.ANY)] * (n_w + n_out)
        + [pl.BlockSpec(memory_space=pltpu.VMEM)] * len(tails),
        out_specs=[pl.BlockSpec(memory_space=pl.ANY)] * n_out,
        out_shape=[jax.ShapeDtypeStruct((height, width), BF16)] * n_out,
        scratch_shapes=[
            pltpu.VMEM((n_w, cols, kv), BF16),
            pltpu.VMEM((n_out, rows, kv), BF16),
            pltpu.VMEM((n_out, n_w, height, cols), BF16),
            pltpu.SemaphoreType.DMA((n_w,)),
            pltpu.SemaphoreType.DMA((n_out,)),
            pltpu.SemaphoreType.DMA((n_out, n_w)),
        ],
        compiler_params=PARAMS,
        cost_estimate=cost(
            2 * n_out * height * kv * width, 2 * (n_out * height * (kv + width) + kv * width)
        ),
    )(*weights, *stacks, *tails)


def up_by_slot(pieces, places, slots, rank):
    groups = places.shape[0] // len(pieces)
    height, kv = groups * rank // 2, pieces[0].shape[1] // 2

    def body(place_ref, *refs):
        parts, o_ref, acc = refs[:-2], refs[-2], refs[-1]
        acc[...] = jnp.zeros_like(acc)
        for p, part in enumerate(parts):
            for g, term, side, rows in segments(groups, rank):
                place = place_ref[p * groups + g]

                @pl.when(place < slots)
                def _():
                    acc[place, term] += part[rows, side * kv : (side + 1) * kv].astype(F32)

        o_ref[...] = acc[...].astype(BF16)

    in_specs = [pl.BlockSpec(memory_space=pltpu.SMEM)]
    for piece in pieces:
        last = piece.shape[0] // height - 1
        in_specs.append(pl.BlockSpec((height, 2 * kv), lambda i, last=last: (last, 0)))
    return pl.pallas_call(
        body,
        grid=(1,),
        in_specs=in_specs,
        out_specs=pl.BlockSpec((slots, rank, kv), lambda i: (0, 0, 0)),
        out_shape=jax.ShapeDtypeStruct((slots, rank, kv), BF16),
        scratch_shapes=[pltpu.VMEM((slots, rank, kv), F32)],
        compiler_params=PARAMS,
        cost_estimate=cost(
            len(pieces) * height * kv, 2 * (2 * len(pieces) * height + slots * rank) * kv
        ),
    )(places, *pieces)


def owners_sums(parts, tenants, n_tenants, by_slot, from_up):
    n, groups, rank, cols = parts.shape
    per, _, kv = from_up[0].shape
    r = rank // per
    scale = ADAPTER_SCALE / GROUP_ROWS

    def body(t_ref, p_ref, *refs):
        down_ref, up_ref = refs[-2:]
        up_ref[...] = sum(block[...].astype(F32) for block in refs[:-2]) * scale
        down_ref[...] = jnp.zeros_like(down_ref)

        @pl.loop(0, n)
        def _(d):
            for g in range(groups):
                down_ref[t_ref[d * groups + g]] += p_ref[d, g].astype(F32) * scale

    slot = pl.BlockSpec((1, rank, kv), lambda i, t: (i, 0, 0))
    return pl.pallas_call(
        body,
        grid_spec=pltpu.PrefetchScalarGridSpec(
            num_scalar_prefetch=1,
            grid=(per,),
            in_specs=[pl.BlockSpec((n, groups, r, cols), lambda i, t: (0, 0, i, 0))]
            + [slot] * (1 + len(from_up)),
            out_specs=[pl.BlockSpec((n_tenants, r, cols), lambda i, t: (0, i, 0)), slot],
        ),
        out_shape=[
            jax.ShapeDtypeStruct((n_tenants, rank, cols), F32),
            jax.ShapeDtypeStruct((per, rank, kv), F32),
        ],
        compiler_params=PARAMS,
        cost_estimate=cost(
            n * groups * rank * cols, 2 * n * groups * rank * cols + 4 * n_tenants * rank * cols
        ),
    )(tenants, parts, by_slot, *from_up)


def input_gradient(pieces, blocks, low, down):
    n, groups, rank, cols = down.shape
    per = n // len(pieces)
    width = n * cols

    def body(b_ref, low_ref, a_ref, *refs):
        o_ref = refs[-1]
        for p, f_ref in enumerate(refs[:-1]):
            for i in range(per):
                block = b_ref[p * per + i]
                adapter = jnp.dot(low_ref[0], a_ref[block, 0], preferred_element_type=F32)
                place = pl.ds(pl.multiple_of(block * cols, cols), cols)
                frozen = f_ref[:, i * cols : (i + 1) * cols].astype(F32)
                o_ref[:, place] = (frozen + ADAPTER_SCALE * adapter).astype(BF16)

    return pl.pallas_call(
        body,
        grid_spec=pltpu.PrefetchScalarGridSpec(
            num_scalar_prefetch=1,
            grid=(groups,),
            in_specs=[
                pl.BlockSpec((1, GROUP_ROWS, rank), lambda g, b: (g, 0, 0)),
                pl.BlockSpec((n, 1, rank, cols), lambda g, b: (0, g, 0, 0)),
            ]
            + [pl.BlockSpec((GROUP_ROWS, per * cols), lambda g, b: (g, 0)) for _ in pieces],
            out_specs=pl.BlockSpec((GROUP_ROWS, width), lambda g, b: (g, 0)),
        ),
        out_shape=jax.ShapeDtypeStruct((groups * GROUP_ROWS, width), BF16),
        compiler_params=PARAMS,
        cost_estimate=cost(
            2 * groups * GROUP_ROWS * rank * width,
            2 * groups * (2 * GROUP_ROWS + rank) * width,
        ),
    )(blocks, low, down, *pieces)


def local(
    layer_input, value_grad, frozen_weight, adapter_down, adapter_up, group_tenant, slot_tenant
):
    x = layer_input[0]
    v = value_grad[0]
    w = frozen_weight[0]
    down = jnp.swapaxes(adapter_down[0], 1, 2)
    up = adapter_up[0]
    tenants = group_tenant[0]
    n = lax.axis_size("dp")
    me = lax.axis_index("dp")
    rows, kv = v.shape
    n_tenants, rank, cols = down.shape
    groups = rows // GROUP_ROWS
    my_tenants = lax.dynamic_slice_in_dim(tenants, me * groups, groups)

    w_own, w_below, w_above = (move(w, "col", step, 1) for step in (0, 1, -1))
    weights = (w_own, w_below, w_above, move(w_own, "col", 2))
    v_next = to_previous_section(v)

    down_mine = exchange(down[tenants].reshape(n, groups, rank, cols))

    low = jnp.einsum(
        "gnk,grk->gnr",
        v.reshape(groups, GROUP_ROWS, kv),
        up[my_tenants],
        preferred_element_type=F32,
    ).astype(BF16)
    v_below, v_above, v_far = (move(v_next, "row", step) for step in (1, -1, 2))
    parts = up_parts(x, down_mine, v)
    for_above, for_below = frozen_terms((v_above, v_below), weights, parts)
    from_below, from_above = move(for_above, "row", 1), move(for_below, "row", -1)
    (for_far,) = frozen_terms((v_far,), weights, parts)
    low, for_above = together(low, for_above)
    low_next = to_previous_section(low)
    down_mine, low_next = together(down_mine, low_next)
    down_next = to_previous_section(down_mine)
    from_far = move(for_far, "row", 2)
    low, for_far = together(low, for_far)
    sent = group_terms(x, jnp.swapaxes(low, 1, 2))
    (own,) = frozen_terms((v_next,), weights)
    sent, from_below, from_above, from_far, own = together(
        sent, from_below, from_above, from_far, own
    )
    terms = exchange(sent)

    odd = lax.axis_index("section") % 2 == 1
    mz, mx = me // RING, me % RING
    row, col = jnp.where(odd, mz, mx), jnp.where(odd, mx, mz)

    def device_at(r, c):
        return jnp.where(odd, RING * r + c, RING * c + r).astype(jnp.int32)

    steps = jnp.array([0, -1, 1, 2])
    per = n_tenants // n
    holders = device_at((row + steps) % RING, col)
    held = tenants.reshape(n, groups)[holders].reshape(-1)
    owners = device_at(row, (col + steps) % RING)
    wanted = slot_tenant.reshape(n, per)[owners].reshape(-1)
    matches = held[:, None] == wanted[None, :]
    places = jnp.where(jnp.any(matches, 1), jnp.argmax(matches, 1), wanted.shape[0])
    by_slot = up_by_slot(
        (parts, from_below, from_above, from_far),
        places.astype(jnp.int32),
        RING * per,
        rank,
    )
    _, to_below, to_above, to_far = by_slot.reshape(RING, per, rank, kv)
    from_up = (move(to_below, "col", -1), move(to_above, "col", 1), move(to_far, "col", 2))

    blocks = jnp.concatenate(
        [device_at((row + step) % RING, (col + steps) % RING) for step in (0, -1, 1, 2)]
    )
    out = input_gradient((own, from_below, from_above, from_far), blocks, low_next, down_next)
    out, terms, *from_up = together(out, terms, *from_up)
    down_grad, up_grad = owners_sums(terms, tenants, n_tenants, by_slot, from_up)
    return (out[None], jnp.swapaxes(down_grad, 1, 2)[None], up_grad[None])


def solution(mesh):
    placed = (
        P("section", "dp", None),
        P("section", "dp", None),
        P("section", "dp", None),
        P("section", None, "dp", None),
        P("section", None, None, None),
        P("section", None),
        P(),
    )
    return jax.shard_map(
        local,
        mesh=mesh,
        in_specs=placed,
        out_specs=(
            P("section", "dp", None),
            P("section", None, "dp", None),
            P("section", "dp", None, None),
        ),
        check_vma=False,
    )
```

```python
import jax
import jax.numpy as jnp
from jax import lax
from jax.experimental import pallas as pl
from jax.experimental.pallas import tpu as pltpu
from jax.sharding import PartitionSpec as P

GROUP_ROWS = 128
ADAPTER_SCALE = 2.0
WIDE = 4
PARAMS = pltpu.CompilerParams(vmem_limit_bytes=58 * 2**20)
RING = 4

F32 = jnp.float32
BF16 = jnp.bfloat16
NT = (((1,), (1,)), ((), ()))


def dot(a, b, dims):
    return lax.dot_general(a, b, dims, preferred_element_type=F32)


def cost(flops, nbytes):
    return pl.CostEstimate(flops=int(flops), bytes_accessed=int(nbytes), transcendentals=0)


def to_previous_section(block):
    n = lax.axis_size("section")
    return lax.ppermute(block, "section", [(i, i - 1) for i in range(1, n)])


def along(axis, distance, down):
    route = []
    for section in range(lax.axis_size("section") - down):
        for z in range(RING):
            for x in range(RING):
                if (axis == "row") == (section % 2 == 0):
                    to = (z, (x + distance) % RING)
                else:
                    to = ((z + distance) % RING, x)
                base = RING * RING * section
                start = base + RING * RING * down + RING * z + x
                route.append((start, base + RING * to[0] + to[1]))
    return route


def move(block, axis, distance, down=0):
    return lax.ppermute(block, ("section", "dp"), along(axis, distance, down))


def exchange(blocks):
    return lax.all_to_all(blocks, "dp", split_axis=0, concat_axis=0, tiled=True)


def together(*values):
    return lax.optimization_barrier(values)


def group_terms(x, low_t):
    rows, width = x.shape
    groups, rank, _ = low_t.shape
    n = lax.axis_size("dp")
    cols = width // n

    def body(x_ref, low_ref, o_ref):
        for q in range(WIDE):
            for g in range(groups):
                o_ref[q, g] = jnp.dot(
                    low_ref[g],
                    x_ref[g * GROUP_ROWS : (g + 1) * GROUP_ROWS, q * cols : (q + 1) * cols],
                    preferred_element_type=F32,
                ).astype(BF16)

    return pl.pallas_call(
        body,
        grid=(n // WIDE,),
        in_specs=[
            pl.BlockSpec((rows, WIDE * cols), lambda d: (0, d)),
            pl.BlockSpec((groups, rank, GROUP_ROWS), lambda d: (0, 0, 0)),
        ],
        out_specs=pl.BlockSpec((WIDE, groups, rank, cols), lambda d: (d, 0, 0, 0)),
        out_shape=jax.ShapeDtypeStruct((n, groups, rank, cols), BF16),
        compiler_params=PARAMS,
        cost_estimate=cost(2 * rows * width * rank, 2 * (rows * width + groups * rank * width)),
    )(x, low_t)


def segments(groups, rank):
    half = groups * rank // 2
    out = []
    for g in range(groups):
        start, stop = g * rank, (g + 1) * rank
        for side in range(2):
            lo, hi = max(start, side * half), min(stop, (side + 1) * half)
            if lo < hi:
                out.append((g, slice(lo - start, hi - start), side, slice(lo - side * half, hi - side * half)))
    return out


def up_parts(x, down, v):
    rows, width = x.shape
    n, groups, rank, cols = down.shape
    kv = v.shape[1]

    def body(x_ref, a_ref, v_ref, o_ref, acc):
        d = pl.program_id(0)

        @pl.when(d == 0)
        def _():
            acc[...] = jnp.zeros_like(acc)

        for g in range(groups):
            span = slice(g * GROUP_ROWS, (g + 1) * GROUP_ROWS)
            for q in range(WIDE):
                acc[:, span] += dot(a_ref[q, g], x_ref[span, q * cols : (q + 1) * cols], NT)

        @pl.when(d == n // WIDE - 1)
        def _():
            for g, term, side, place in segments(groups, rank):
                span = slice(g * GROUP_ROWS, (g + 1) * GROUP_ROWS)
                o_ref[place, side * kv : (side + 1) * kv] = jnp.dot(
                    acc[term, span].astype(BF16), v_ref[span, :], preferred_element_type=F32
                ).astype(BF16)

    return pl.pallas_call(
        body,
        grid=(n // WIDE,),
        in_specs=[
            pl.BlockSpec((rows, WIDE * cols), lambda d: (0, d)),
            pl.BlockSpec((WIDE, groups, rank, cols), lambda d: (d, 0, 0, 0)),
            pl.BlockSpec((rows, kv), lambda d: (0, 0)),
        ],
        out_specs=pl.BlockSpec((groups * rank // 2, 2 * kv), lambda d: (0, 0)),
        out_shape=jax.ShapeDtypeStruct((groups * rank // 2, 2 * kv), BF16),
        scratch_shapes=[pltpu.VMEM((rank, rows), F32)],
        compiler_params=PARAMS,
        cost_estimate=cost(2 * rows * width * rank, 2 * (rows * width + groups * rank * width)),
    )(x, down, v)


def frozen_terms(stacks, weights, tail=None):
    kv = weights[0].shape[1]
    rows = stacks[0].shape[0]
    n_w, n_out = len(weights), len(stacks)
    cols = weights[0].shape[0]
    extra = 0 if tail is None else tail.shape[0]
    height, width = rows + extra, n_w * cols
    tails = [] if tail is None else [tail]

    def body(*refs):
        w_hbm, refs = refs[:n_w], refs[n_w:]
        v_hbm, refs = refs[:n_out], refs[n_out:]
        tail_refs, refs = refs[: len(tails)], refs[len(tails) :]
        out_hbm, refs = refs[:n_out], refs[n_out:]
        w_vmem, v_vmem, out_vmem, w_sem, v_sem, out_sem = refs
        w_loads = [
            pltpu.make_async_copy(w_hbm[q], w_vmem.at[q], w_sem.at[q]) for q in range(n_w)
        ]
        v_loads = [
            pltpu.make_async_copy(v_hbm[i], v_vmem.at[i], v_sem.at[i]) for i in range(n_out)
        ]
        w_loads[0].start()
        for load in v_loads + w_loads[1:2]:
            load.start()
        stores = []
        for q in range(n_w):
            w_loads[q].wait()
            if q + 2 < n_w:
                w_loads[q + 2].start()
            span = slice(q * cols, (q + 1) * cols)
            for i in range(n_out):
                if q == 0:
                    v_loads[i].wait()
                out_vmem[i, q, :rows, :] = dot(v_vmem[i], w_vmem[q], NT).astype(BF16)
                if tail_refs:
                    out_vmem[i, q, rows:, :] = tail_refs[0][:, span]
                store = pltpu.make_async_copy(
                    out_vmem.at[i, q], out_hbm[i].at[:, span], out_sem.at[i, q]
                )
                store.start()
                stores.append(store)
        for store in stores:
            store.wait()

    return pl.pallas_call(
        body,
        in_specs=[pl.BlockSpec(memory_space=pl.ANY)] * (n_w + n_out)
        + [pl.BlockSpec(memory_space=pltpu.VMEM)] * len(tails),
        out_specs=[pl.BlockSpec(memory_space=pl.ANY)] * n_out,
        out_shape=[jax.ShapeDtypeStruct((height, width), BF16)] * n_out,
        scratch_shapes=[
            pltpu.VMEM((n_w, cols, kv), BF16),
            pltpu.VMEM((n_out, rows, kv), BF16),
            pltpu.VMEM((n_out, n_w, height, cols), BF16),
            pltpu.SemaphoreType.DMA((n_w,)),
            pltpu.SemaphoreType.DMA((n_out,)),
            pltpu.SemaphoreType.DMA((n_out, n_w)),
        ],
        compiler_params=PARAMS,
        cost_estimate=cost(
            2 * n_out * height * kv * width, 2 * (n_out * height * (kv + width) + kv * width)
        ),
    )(*weights, *stacks, *tails)


def up_by_slot(pieces, places, slots, rank):
    groups = places.shape[0] // len(pieces)
    height, kv = groups * rank // 2, pieces[0].shape[1] // 2

    def body(place_ref, *refs):
        parts, o_ref, acc = refs[:-2], refs[-2], refs[-1]
        acc[...] = jnp.zeros_like(acc)
        for p, part in enumerate(parts):
            for g, term, side, rows in segments(groups, rank):
                place = place_ref[p * groups + g]

                @pl.when(place < slots)
                def _():
                    acc[place, term] += part[rows, side * kv : (side + 1) * kv].astype(F32)

        o_ref[...] = acc[...].astype(BF16)

    in_specs = [pl.BlockSpec(memory_space=pltpu.SMEM)]
    for piece in pieces:
        last = piece.shape[0] // height - 1
        in_specs.append(pl.BlockSpec((height, 2 * kv), lambda i, last=last: (last, 0)))
    return pl.pallas_call(
        body,
        grid=(1,),
        in_specs=in_specs,
        out_specs=pl.BlockSpec((slots, rank, kv), lambda i: (0, 0, 0)),
        out_shape=jax.ShapeDtypeStruct((slots, rank, kv), BF16),
        scratch_shapes=[pltpu.VMEM((slots, rank, kv), F32)],
        compiler_params=PARAMS,
        cost_estimate=cost(
            len(pieces) * height * kv, 2 * (2 * len(pieces) * height + slots * rank) * kv
        ),
    )(places, *pieces)


def owners_sums(parts, tenants, n_tenants, by_slot, from_up):
    n, groups, rank, cols = parts.shape
    per, _, kv = from_up[0].shape
    r = rank // per
    scale = ADAPTER_SCALE / GROUP_ROWS

    def body(t_ref, p_ref, *refs):
        down_ref, up_ref = refs[-2:]
        up_ref[...] = sum(block[...].astype(F32) for block in refs[:-2]) * scale
        down_ref[...] = jnp.zeros_like(down_ref)

        @pl.loop(0, n)
        def _(d):
            for g in range(groups):
                down_ref[t_ref[d * groups + g]] += p_ref[d, g].astype(F32) * scale

    slot = pl.BlockSpec((1, rank, kv), lambda i, t: (i, 0, 0))
    return pl.pallas_call(
        body,
        grid_spec=pltpu.PrefetchScalarGridSpec(
            num_scalar_prefetch=1,
            grid=(per,),
            in_specs=[pl.BlockSpec((n, groups, r, cols), lambda i, t: (0, 0, i, 0))]
            + [slot] * (1 + len(from_up)),
            out_specs=[pl.BlockSpec((n_tenants, r, cols), lambda i, t: (0, i, 0)), slot],
        ),
        out_shape=[
            jax.ShapeDtypeStruct((n_tenants, rank, cols), F32),
            jax.ShapeDtypeStruct((per, rank, kv), F32),
        ],
        compiler_params=PARAMS,
        cost_estimate=cost(
            n * groups * rank * cols, 2 * n * groups * rank * cols + 4 * n_tenants * rank * cols
        ),
    )(tenants, parts, by_slot, *from_up)


def input_gradient(pieces, blocks, low, down):
    n, groups, rank, cols = down.shape
    per = n // len(pieces)
    width = n * cols

    def body(b_ref, low_ref, a_ref, *refs):
        o_ref = refs[-1]
        for p, f_ref in enumerate(refs[:-1]):
            for i in range(per):
                block = b_ref[p * per + i]
                adapter = jnp.dot(low_ref[0], a_ref[block, 0], preferred_element_type=F32)
                place = pl.ds(pl.multiple_of(block * cols, cols), cols)
                frozen = f_ref[:, i * cols : (i + 1) * cols].astype(F32)
                o_ref[:, place] = (frozen + ADAPTER_SCALE * adapter).astype(BF16)

    return pl.pallas_call(
        body,
        grid_spec=pltpu.PrefetchScalarGridSpec(
            num_scalar_prefetch=1,
            grid=(groups,),
            in_specs=[
                pl.BlockSpec((1, GROUP_ROWS, rank), lambda g, b: (g, 0, 0)),
                pl.BlockSpec((n, 1, rank, cols), lambda g, b: (0, g, 0, 0)),
            ]
            + [pl.BlockSpec((GROUP_ROWS, per * cols), lambda g, b: (g, 0)) for _ in pieces],
            out_specs=pl.BlockSpec((GROUP_ROWS, width), lambda g, b: (g, 0)),
        ),
        out_shape=jax.ShapeDtypeStruct((groups * GROUP_ROWS, width), BF16),
        compiler_params=PARAMS,
        cost_estimate=cost(
            2 * groups * GROUP_ROWS * rank * width,
            2 * groups * (2 * GROUP_ROWS + rank) * width,
        ),
    )(blocks, low, down, *pieces)


def local(
    layer_input, value_grad, frozen_weight, adapter_down, adapter_up, group_tenant, slot_tenant
):
    x = layer_input[0]
    v = value_grad[0]
    w = frozen_weight[0]
    down = jnp.swapaxes(adapter_down[0], 1, 2)
    up = adapter_up[0]
    tenants = group_tenant[0]
    n = lax.axis_size("dp")
    me = lax.axis_index("dp")
    rows, kv = v.shape
    n_tenants, rank, cols = down.shape
    groups = rows // GROUP_ROWS
    my_tenants = lax.dynamic_slice_in_dim(tenants, me * groups, groups)

    w_own, w_below, w_above = (move(w, "col", step, 1) for step in (0, 1, -1))
    weights = (w_own, w_below, w_above, move(w_own, "col", 2))
    v_next = to_previous_section(v)

    down_mine = exchange(down[tenants].reshape(n, groups, rank, cols))

    low = jnp.einsum(
        "gnk,grk->gnr",
        v.reshape(groups, GROUP_ROWS, kv),
        up[my_tenants],
        preferred_element_type=F32,
    ).astype(BF16)
    v_below, v_above, v_far = (move(v_next, "row", step) for step in (1, -1, 2))
    parts = up_parts(x, down_mine, v)
    for_above, for_below = frozen_terms((v_above, v_below), weights, parts)
    from_below, from_above = move(for_above, "row", 1), move(for_below, "row", -1)
    (for_far,) = frozen_terms((v_far,), weights, parts)
    down_mine, low, for_above = together(down_mine, low, for_above)
    down_next = to_previous_section(down_mine)
    low_next = to_previous_section(low)
    from_far = move(for_far, "row", 2)
    low, for_far = together(low, for_far)
    sent = group_terms(x, jnp.swapaxes(low, 1, 2))
    (own,) = frozen_terms((v_next,), weights)
    sent, from_below, from_above, from_far, own = together(
        sent, from_below, from_above, from_far, own
    )
    terms = exchange(sent)

    odd = lax.axis_index("section") % 2 == 1
    mz, mx = me // RING, me % RING
    row, col = jnp.where(odd, mz, mx), jnp.where(odd, mx, mz)

    def device_at(r, c):
        return jnp.where(odd, RING * r + c, RING * c + r).astype(jnp.int32)

    steps = jnp.array([0, -1, 1, 2])
    per = n_tenants // n
    holders = device_at((row + steps) % RING, col)
    held = tenants.reshape(n, groups)[holders].reshape(-1)
    owners = device_at(row, (col + steps) % RING)
    wanted = slot_tenant.reshape(n, per)[owners].reshape(-1)
    matches = held[:, None] == wanted[None, :]
    places = jnp.where(jnp.any(matches, 1), jnp.argmax(matches, 1), wanted.shape[0])
    by_slot = up_by_slot(
        (parts, from_below, from_above, from_far),
        places.astype(jnp.int32),
        RING * per,
        rank,
    )
    _, to_below, to_above, to_far = by_slot.reshape(RING, per, rank, kv)
    from_up = (move(to_below, "col", -1), move(to_above, "col", 1), move(to_far, "col", 2))

    blocks = jnp.concatenate(
        [device_at((row + step) % RING, (col + steps) % RING) for step in (0, -1, 1, 2)]
    )
    out = input_gradient((own, from_below, from_above, from_far), blocks, low_next, down_next)
    out, terms, *from_up = together(out, terms, *from_up)
    down_grad, up_grad = owners_sums(terms, tenants, n_tenants, by_slot, from_up)
    return (out[None], jnp.swapaxes(down_grad, 1, 2)[None], up_grad[None])


def solution(mesh):
    placed = (
        P("section", "dp", None),
        P("section", "dp", None),
        P("section", "dp", None),
        P("section", None, "dp", None),
        P("section", None, None, None),
        P("section", None),
        P(),
    )
    return jax.shard_map(
        local,
        mesh=mesh,
        in_specs=placed,
        out_specs=(
            P("section", "dp", None),
            P("section", None, "dp", None),
            P("section", "dp", None, None),
        ),
        check_vma=False,
    )
```
